32 devices in a mesh: rows: 8 (over z, core), cols: 4 (over y, x).
Axes of the slice: x: 2, y: 2, z: 4, core: 2. Of those that a mesh axis runs over, the one named last changes fastest.
Arguments:
- window_slab: float32 [24576, 4096], P('rows', 'cols'), may hold values from -6 to 6
- first_inverse: float32 [2, 512, 512], replicated, may hold values from -2 to 2, as said below
- first_factor: float32 [2, 512, 24576], P(None, 'cols', 'rows'), may hold values from -0.25 to 0.25
- second_inverse: float32 [2, 512, 512], replicated, may hold values from -2 to 2, as said below
- second_factor: float32 [2, 512, 4096], P(None, 'cols', 'rows'), may hold values from -0.25 to 0.25
Outputs:
- reduced: float32 [24576, 4096], P('cols', 'rows')
The draws below stay inside these ranges and needn't reach their ends.
Inputs may be any that keep to these rules, and one draw needn't show every extreme that they name: first_inverse[k] is lower triangular with diagonal entries from 0.5 to 2. second_inverse[k] is lower triangular with diagonal entries from 0.5 to 2.
All inputs are finite; a program needn't handle non-finite values.
Results may differ from the reference program's by a relative error of at most 0.0001.
Values sent between devices are 32-bit elements; how exact they have to be, the bound alone decides.
No kernel may reach another device: no remote copies, remote signals or barrier semaphores. Data moves between devices by JAX's collectives and lax.ppermute only.
A program may use at most 128 MiB of HBM per device.

```python
import math
import jax
import jax.numpy as jnp
from jax import lax

ORDER = 24576
WIDTH = 4096
PANEL = 512
BLOCK = 128
PANELS = 2
ROW_SHARE = 3072
PIECE = 768
N_ROWS = 8
N_COLS = 4


def triangle(key, salt):
    folded = jax.random.fold_in(key, salt)
    diag_key, off_key = jax.random.split(folded)
    shape = (PANELS, PANEL, PANEL)
    diagonal = jnp.exp(jax.random.uniform(diag_key, shape, jnp.float32, math.log(0.5), math.log(2.0)))
    offdiag = jnp.clip(jax.random.normal(off_key, shape, jnp.float32), -4.0, 4.0) * 0.7 / math.sqrt(PANEL)
    row_ids = lax.broadcasted_iota(jnp.int32, shape, 1)
    col_ids = lax.broadcasted_iota(jnp.int32, shape, 2)
    return jnp.where(row_ids == col_ids, diagonal, jnp.where(row_ids > col_ids, offdiag, 0.0)).astype(jnp.float32)


def draw_first_inverse(key, part):
    return triangle(key, 11)


def draw_second_inverse(key, part):
    return triangle(key, 23)


def shard_levels(rng, shape, pieces, low, top_value):
    level = 1.0
    for position, blocks in pieces:
        heights = jax.random.uniform(jax.random.fold_in(jax.random.fold_in(rng, 6), position), (blocks,), jnp.float32, low / len(pieces), top_value / len(pieces))
        level = level * jnp.repeat(jnp.exp(heights), shape[position] // blocks).reshape((-1,) + (1,) * (len(shape) - 1 - position))
    return level


def centred(own_key, extent, spread, most, cuts=(), held_as=jnp.bfloat16):
    drawn = jax.random.normal(own_key, extent, jnp.float32) * spread
    if len(cuts) > 0:
        drawn = shard_levels(own_key, extent, cuts, -0.22, 0.18) * drawn
    return jnp.clip(drawn, min=-most, max=most).astype(held_as)


def setup_inputs(seed: int = 0) -> dict:
    key_of = jax.random.split(jax.random.key(seed), 6)
    window_slab = centred(key_of[0], (ORDER, WIDTH), 1.0, 6.0, ((0, 8), (1, 4)), jnp.float32)
    first_inverse = draw_first_inverse(jax.random.fold_in(key_of[5], 71), 0)
    first_factor = centred(key_of[2], (PANELS, PANEL, ORDER), PANEL ** -0.5, 0.25, ((1, 4), (2, 8)), jnp.float32)
    second_inverse = draw_second_inverse(jax.random.fold_in(key_of[5], 71), 0)
    second_factor = centred(key_of[4], (PANELS, PANEL, WIDTH), PANEL ** -0.5, 0.25, ((1, 4), (2, 8)), jnp.float32)
    return {"window_slab": window_slab, "first_inverse": first_inverse, "first_factor": first_factor, "second_inverse": second_inverse, "second_factor": second_factor}


HIGHEST = lax.Precision.HIGHEST


def to_logical(stored):
    trailing = stored.shape[1]
    return stored.reshape(N_ROWS, ROW_SHARE // BLOCK, BLOCK, trailing).transpose(1, 0, 2, 3).reshape(ORDER, trailing)


def to_stored(logical):
    trailing = logical.shape[1]
    return logical.reshape(ROW_SHARE // BLOCK, N_ROWS, BLOCK, trailing).transpose(1, 0, 2, 3).reshape(ORDER, trailing)


def reference(window_slab, first_inverse, first_factor, second_inverse, second_factor):
    current = to_logical(window_slab)
    factors = to_logical(first_factor.transpose(2, 0, 1).reshape(ORDER, PANELS * PANEL))
    for panel_index in range(PANELS):
        panel_start = panel_index * PANEL
        panel_end = panel_start + PANEL
        solved = jnp.dot(first_inverse[panel_index], current[panel_start:panel_end], precision=HIGHEST, preferred_element_type=jnp.float32)
        update = jnp.dot(factors[panel_end:, panel_start:panel_end], solved, precision=HIGHEST, preferred_element_type=jnp.float32)
        current = jnp.concatenate([current[:panel_start], solved, current[panel_end:] - update], axis=0)
    turned = to_stored(current).reshape(N_ROWS, N_COLS, PIECE, WIDTH).transpose(1, 0, 2, 3).reshape(ORDER, WIDTH)
    for panel_index in range(PANELS):
        panel_start = panel_index * PANEL
        panel_end = panel_start + PANEL
        solved = jnp.dot(turned[:, panel_start:panel_end], second_inverse[panel_index].T, precision=HIGHEST, preferred_element_type=jnp.float32)
        update = jnp.dot(solved, second_factor[panel_index][:, panel_end:], precision=HIGHEST, preferred_element_type=jnp.float32)
        turned = jnp.concatenate([turned[:, :panel_start], solved, turned[:, panel_end:] - update], axis=1)
    return turned
```

```python
import functools

import jax
import jax.numpy as jnp
from jax import lax
from jax.experimental import pallas as pl
from jax.experimental.pallas import tpu as pltpu
from jax.sharding import PartitionSpec as P

BLOCK = 128
AHEAD = 2
SHARE = 1000
PLAIN = (((1,), (0,)), ((), ()))
CONTRACT_COLS = (((1,), (1,)), ((), ()))
ANY = pl.BlockSpec(memory_space=pl.ANY)


def split(value):
    high = value.astype(jnp.bfloat16)
    low = (value - high.astype(jnp.float32)).astype(jnp.bfloat16)
    return high, low


def product(left, right, contract=PLAIN):
    def one(a, b):
        return lax.dot_general(a, b, contract, preferred_element_type=jnp.float32)

    return one(left[0], right[0]) + (one(left[0], right[1]) + one(left[1], right[0]))


def whole(shape):
    return pl.BlockSpec(shape, lambda *_: (0,) * len(shape))


def cost(flops, read):
    return pl.CostEstimate(flops=flops // SHARE, bytes_accessed=read // SHARE, transcendentals=0)


def compiler_params(mib):
    return pltpu.CompilerParams(vmem_limit_bytes=mib * 2**20)


def solve_kernel(panels, place, own, other, inverse_ref, corner_ref, *refs):
    solved_ref, high_ref, low_ref, head, inv_high, inv_low, cor_high, cor_low = refs
    width = inverse_ref.shape[1]
    blocks = width // BLOCK

    @pl.when(pl.program_id(0) == 0)
    def _():
        for k in range(panels):
            inv_high[k], inv_low[k] = split(inverse_ref[k])
            for p in range(k):
                for b in range(blocks):
                    rows = slice((k * blocks + b) * BLOCK, (k * blocks + b + 1) * BLOCK)
                    for c in range(corner_ref.shape[0]):
                        parts = split(corner_ref[c, (k - 1) * blocks + b, p].T)
                        held = corner_ref.shape[3]
                        columns = slice(c * held, (c + 1) * held)
                        cor_high[p, rows, columns], cor_low[p, rows, columns] = parts

    for b in range(panels * blocks):
        mine = jnp.where(place[0] == b % 2, own[b // 2], other[b // 2])
        head[b * BLOCK : (b + 1) * BLOCK] = mine
    parts = []
    for k in range(panels):
        rows = slice(k * width, (k + 1) * width)
        current = head[rows]
        for p in range(k):
            block = (cor_high[p, rows], cor_low[p, rows])
            current = current - product(block, parts[p])
        answer = product((inv_high[k], inv_low[k]), split(current))
        parts.append(split(answer))
        solved_ref[rows] = answer
        high_ref[rows] = parts[k][0]
        low_ref[rows] = parts[k][1]


def solve_rows(place, own, other, inverse, corner):
    panels, width, _ = inverse.shape
    breadth = own.shape[2]
    depth = panels * width
    tile = min(breadth, 256)
    half = pl.BlockSpec((depth // BLOCK // 2, BLOCK, tile), lambda i, _: (0, 0, i))
    block = pl.BlockSpec((depth, tile), lambda i, _: (0, i))
    corner_shape = (panels - 1, depth, width)
    return pl.pallas_call(
        functools.partial(solve_kernel, panels),
        grid_spec=pltpu.PrefetchScalarGridSpec(
            num_scalar_prefetch=1,
            grid=(breadth // tile,),
            in_specs=[half, half, whole(inverse.shape), whole(corner.shape)],
            out_specs=[block] * 3,
            scratch_shapes=[
                pltpu.VMEM((depth, tile), jnp.float32),
                pltpu.VMEM(inverse.shape, jnp.bfloat16),
                pltpu.VMEM(inverse.shape, jnp.bfloat16),
                pltpu.VMEM(corner_shape, jnp.bfloat16),
                pltpu.VMEM(corner_shape, jnp.bfloat16),
            ],
        ),
        out_shape=[
            jax.ShapeDtypeStruct((depth, breadth), t)
            for t in (jnp.float32, jnp.bfloat16, jnp.bfloat16)
        ],
        compiler_params=compiler_params(60),
        cost_estimate=cost(6 * 3 * width * width * breadth, 16 * depth * breadth),
        name="solve_rows",
    )(place, own, other, inverse, corner)


def update_kernel(tops, slots, offset, count, place, slab, *rest):
    factors = rest[:count]
    high, low, own_top = rest[count : count + 3]
    outs = rest[-slots - 3 : -3]
    factor_high, factor_low, total = rest[-3:]

    @pl.when(pl.program_id(0) == 0)
    def _():
        panels, share, columns = factors[0].shape
        held = columns // slots
        chunk = slab.shape[1]
        for dest in range(slots):
            rows = slice(dest * chunk, (dest + 1) * chunk)
            taken = slice(dest * held + offset, dest * held + offset + chunk)
            for panel in range(panels):
                for slot in range(count):
                    start = pl.multiple_of((place[1] ^ slot) * share, BLOCK)
                    at = pl.ds(panel * share * count + start, share)
                    parts = split(factors[slot][panel, :, taken].T)
                    factor_high[rows, at], factor_low[rows, at] = parts

    answer = product((factor_high[...], factor_low[...]), (high[...], low[...]))
    total[...] = answer.reshape(total.shape)
    for dest, first, count, flag in tops:

        @pl.when(place[2 + flag] > 0)
        def _():
            total[dest, :count] = slab[dest, :count] - own_top[first : first + count]

    for slot in range(slots):
        dest = place[0] ^ slot
        outs[slot][...] = slab[dest] - total[dest]


def update_rows(place, slab, factors, high, low, own_top, begin, chunk, offset, after):
    slots, piece, breadth = slab.shape
    depth = high.shape[0]
    tile = min(breadth, 256)
    assert begin % chunk == 0
    tops = []
    for dest in range(slots):
        first = dest * piece + begin
        for b in range(own_top.shape[0] // BLOCK):
            start, stop = max(first, b * BLOCK), min(first + chunk, (b + 1) * BLOCK)
            if start < stop:
                assert start == first
                tops.append((dest, start, stop - start, b))
    columns = pl.BlockSpec((depth, tile), lambda i, _: (0, i))
    return pl.pallas_call(
        functools.partial(update_kernel, tops, slots, offset, len(factors)),
        grid_spec=pltpu.PrefetchScalarGridSpec(
            num_scalar_prefetch=1,
            grid=(breadth // tile,),
            in_specs=[
                pl.BlockSpec((slots, chunk, tile), lambda i, _: (0, begin // chunk, i)),
                *[whole(f.shape) for f in factors],
                columns,
                columns,
                pl.BlockSpec((own_top.shape[0], tile), lambda i, _: (0, i)),
            ]
            + [ANY] * len(after),
            out_specs=[pl.BlockSpec((chunk, tile), lambda i, _: (0, i))] * slots,
            scratch_shapes=[
                pltpu.VMEM((slots * chunk, depth), jnp.bfloat16),
                pltpu.VMEM((slots * chunk, depth), jnp.bfloat16),
                pltpu.VMEM((slots, chunk, tile), jnp.float32),
            ],
        ),
        out_shape=[jax.ShapeDtypeStruct((chunk, breadth), jnp.float32)] * slots,
        compiler_params=compiler_params(60),
        cost_estimate=cost(12 * slots * chunk * depth * breadth, 12 * depth * breadth),
        name="update_rows",
    )(place, slab, *factors, high, low, own_top, *after)


def reduce_kernel(slots, views, extra, place, *refs):
    pieces = refs[:slots]
    inverse = refs[slots]
    own = refs[slots + 1 : slots + 1 + views]
    other = refs[slots + 1 + views : slots + 1 + 2 * views]
    out, current, high, low, factor_high, factor_low = refs[slots + 1 + 2 * views + extra :]
    step = pl.program_id(0)
    chunk, breadth = pieces[0].shape
    width = inverse.shape[1]
    depth = current.shape[1]
    narrow = out.shape[2]
    span = depth // breadth
    count, _, piece, _ = own[0].shape
    core = place[1]

    for part in range(span):
        for slot in range(slots):

            @pl.when((step * span + part) ^ place[0] == slot)
            def _():
                current[:, part * breadth : (part + 1) * breadth] = pieces[slot][...]

    def load(group, panels):
        for parity in range(2):
            sources = own if parity == group % 2 else other

            @pl.when(core == parity)
            def _():
                for panel in range(panels):
                    for part in range(count):
                        start = panel * width + part * piece
                        rows = slice(start, start + piece)
                        parts = split(sources[group // 2 * 2 + panel][part, 0])
                        factor_high[rows], factor_low[rows] = parts

    def store(value, start):
        for g in range(value.shape[1] // narrow):
            out[start // narrow + g] = value[:, g * narrow : (g + 1) * narrow]

    @pl.when(step == 0)
    def _():
        first = product(split(current[:, :width]), split(inverse[0]), CONTRACT_COLS)
        first_parts = split(first)
        high[:, :width], low[:, :width] = first_parts
        store(first, 0)
        for group in range(width // narrow, depth // narrow):
            load(group, 1)
            columns = slice(group * narrow, (group + 1) * narrow)
            current[:, columns] -= product(first_parts, (factor_high[:width], factor_low[:width]))
        second = product(split(current[:, width:]), split(inverse[1]), CONTRACT_COLS)
        high[:, width:], low[:, width:] = split(second)
        store(second, width)

    @pl.when(step > 0)
    def _():
        for group in range(depth // narrow):
            load(group, 2)
            columns = slice(group * narrow, (group + 1) * narrow)
            part = product((high[...], low[...]), (factor_high[...], factor_low[...]))
            out[group] = current[:, columns] - part


def reduce_columns(place, pieces, inverse, own, other, row_count, after):
    chunk, breadth = pieces[0].shape
    slots = len(pieces)
    panels, width, _ = inverse.shape
    depth = panels * width
    breadth_all = slots * breadth
    narrow = breadth_all // row_count
    span = depth // narrow // 2
    taken = (own.shape[0], 1) + own.shape[2:]

    def view(chip, panel):
        return pl.BlockSpec(
            taken, lambda i, _: (0, jnp.maximum(2 * (span * i + chip) - 1 + panel, 0), 0, 0)
        )

    views = [view(chip, panel) for chip in range(span) for panel in range(2)]
    return pl.pallas_call(
        functools.partial(reduce_kernel, slots, len(views), len(after)),
        grid_spec=pltpu.PrefetchScalarGridSpec(
            num_scalar_prefetch=1,
            grid=(breadth_all // depth,),
            in_specs=[whole(pieces[0].shape)] * slots
            + [whole(inverse.shape)]
            + views * 2
            + [ANY] * len(after),
            out_specs=pl.BlockSpec((depth // narrow, chunk, narrow), lambda i, _: (i, 0, 0)),
            scratch_shapes=[
                pltpu.VMEM((chunk, depth), jnp.float32),
                pltpu.VMEM((chunk, depth), jnp.bfloat16),
                pltpu.VMEM((chunk, depth), jnp.bfloat16),
                pltpu.VMEM((depth, narrow), jnp.bfloat16),
                pltpu.VMEM((depth, narrow), jnp.bfloat16),
            ],
        ),
        out_shape=jax.ShapeDtypeStruct((row_count, chunk, narrow), jnp.float32),
        compiler_params=compiler_params(60),
        cost_estimate=cost(6 * chunk * depth * breadth_all, 4 * depth * breadth_all),
        name="reduce_columns",
    )(place, *pieces, inverse, *[own] * len(views), *[other] * len(views), *after)


def order_kernel(chips, skipped, place, *refs):
    entry = pl.program_id(0)
    for i in range(2 * chips - 1):
        if not skipped:

            @pl.when(entry - place[0] == i - (chips - 1))
            def _():
                refs[-1][0] = refs[i][...]

        else:
            for panel in range(2):
                chip = (entry + 1 - panel) // 2
                held = jnp.logical_and((entry + 1) % 2 == panel, entry > 0)
                first = panel == 0 and entry == 0

                @pl.when(
                    jnp.logical_and(jnp.logical_or(held, first), chip - place[0] == i - (chips - 1))
                )
                def _():
                    refs[-1][0] = refs[i][panel]


def in_order(place, pieces, skipped, after):
    chips = (len(pieces) + 1) // 2
    shape = pieces[0].shape
    entry = shape[1:] if skipped else shape
    count = 2 * chips - 1 if skipped else chips
    return pl.pallas_call(
        functools.partial(order_kernel, chips, skipped),
        grid_spec=pltpu.PrefetchScalarGridSpec(
            num_scalar_prefetch=1,
            grid=(count,),
            in_specs=[whole(shape)] * len(pieces) + [ANY] * len(after),
            out_specs=pl.BlockSpec((1,) + entry, lambda i, _: (i,) + (0,) * len(entry)),
        ),
        out_shape=jax.ShapeDtypeStruct((count,) + entry, jnp.float32),
        compiler_params=compiler_params(60),
        name="in_order",
    )(place, *pieces, *after)


def along_line(block, row_count, skipped, after):
    chips = row_count // 2
    up = [(i, i + 2) for i in range(row_count - 2)]
    down = [(i + 2, i) for i in range(row_count - 2)]
    below, above = [block], [block]
    for _ in range(chips - 1):
        below.append(lax.ppermute(below[-1], "rows", up))
        above.append(lax.ppermute(above[-1], "rows", down))
    place = jnp.stack([lax.axis_index("rows") // 2])
    return in_order(place, below[:0:-1] + above, skipped, after), [below[-1], above[-1]]


def gate_kernel(*refs):
    pass


def gate(value, after):
    return pl.pallas_call(
        gate_kernel,
        in_specs=[ANY] * (1 + len(after)),
        out_specs=ANY,
        out_shape=jax.ShapeDtypeStruct(value.shape, value.dtype),
        input_output_aliases={0: 0},
        compiler_params=compiler_params(60),
        name="gate",
    )(value, *after)


def pick_kernel(axis, count, *refs):
    out = refs[-1]
    extent = out.shape[axis] // count
    for i in range(count):
        at = (slice(None),) * axis + (slice(i * extent, (i + 1) * extent),)
        out[at] = refs[i][...]


def pick_blocks(source, axis, extent, blocks, after):
    ndim = source.ndim

    def sized(size):
        return source.shape[:axis] + (size,) + source.shape[axis + 1 :]

    def spec(place):
        return pl.BlockSpec(sized(extent), lambda _: (0,) * axis + (place,) + (0,) * (ndim - axis - 1))

    result = sized(extent * len(blocks))
    return pl.pallas_call(
        functools.partial(pick_kernel, axis, len(blocks)),
        grid=(1,),
        in_specs=[spec(b) for b in blocks] + [ANY] * len(after),
        out_specs=whole(result),
        out_shape=jax.ShapeDtypeStruct(result, source.dtype),
        compiler_params=compiler_params(60),
        name="pick_blocks",
    )(*[source] * len(blocks), *after)


def on_device(window_slab, first_inverse, first_factor, second_inverse, second_factor):
    row_count = lax.axis_size("rows")
    col_count = lax.axis_size("cols")
    row_index = lax.axis_index("rows")
    col_index = lax.axis_index("cols")
    core = row_index % 2
    row_share, breadth = window_slab.shape
    panels, width, _ = first_inverse.shape
    depth = panels * width
    assert depth <= row_count * BLOCK and panels == 2
    piece = row_share // col_count
    if piece == 6 * BLOCK:
        sizes, groups = [BLOCK] * 6, [[0, 1], [2, 3], [4, 5]]
    else:
        sizes, groups = [piece], [[0]]
    begins = [sum(sizes[:j]) for j in range(len(sizes))]
    chunks = len(sizes)
    narrow = breadth * col_count // row_count
    swap = [(i, i ^ 1) for i in range(row_count)]

    def from_sibling(value):
        return lax.ppermute(value, "rows", swap)

    over_cols = [[(i, i ^ s) for i in range(col_count)] for s in range(col_count)]

    corner = lax.all_gather(first_factor[: panels - 1, :, :BLOCK], "rows")
    corner = lax.all_gather(corner[width // BLOCK : depth // BLOCK], "cols")

    def gather_factor(group, after):
        begin, extent = begins[group[0]], sum(sizes[j] for j in group)
        if piece % BLOCK == 0:
            blocks = [(d * piece + begin) // extent for d in range(col_count)]
            part = pick_blocks(first_factor, 2, extent, blocks, after)
        else:
            columns = [d * piece + begin for d in range(col_count)]
            part = jnp.concatenate([first_factor[:, :, c : c + extent] for c in columns], 2)
        if group[0] == 0 and col_count == 4:
            parts = [lax.ppermute(part, "cols", pairs) for pairs in over_cols[1:]]
            return [part] + parts, col_index
        return [lax.all_gather(part, "cols", axis=1, tiled=True)], 0

    factors = [gather_factor(groups[0], [])]

    line, last = along_line(second_factor, row_count, True, factors[0][0][1:] + [corner])
    own_second = lax.all_gather(line, "cols")

    own_head, _ = along_line(pick_blocks(window_slab, 0, BLOCK, [0], last), row_count, False, [])
    other_head = from_sibling(own_head)
    solved, solved_high, solved_low = solve_rows(
        jnp.stack([core]), own_head, other_head, first_inverse, corner
    )
    start = row_index * BLOCK
    own_top = lax.dynamic_slice_in_dim(solved, jnp.minimum(start, depth - BLOCK), BLOCK, 0)
    is_top = (start < depth).astype(jnp.int32)

    slab = window_slab.reshape(col_count, piece, breadth)
    updated, done, results, ready = [], [], [], []

    def update(j):
        number = next(g for g, group in enumerate(groups) if j in group)
        after = [done[max(j - AHEAD, 1)]] if j >= AHEAD else ready
        arrays, order = factors[number]
        out = update_rows(
            jnp.stack([col_index, jnp.int32(order), is_top]),
            slab,
            arrays,
            solved_high,
            solved_low,
            own_top,
            begins[j],
            sizes[j],
            begins[j] - begins[groups[number][0]],
            after,
        )
        pieces = [out[0]]
        for slot in range(1, col_count):
            pieces.append(lax.ppermute(out[slot], "cols", over_cols[slot]))
        updated.append((out, pieces))

    update(0)

    own_second = gate(own_second, [updated[0][0][0]])
    other_second = from_sibling(own_second)
    place_cores = jnp.stack([col_index, core])
    ready = [own_second]
    if chunks > 1:
        update(1)
    factors += [gather_factor(group, ready) for group in groups[1:]]

    for j in range(chunks):
        pieces = updated[j][1]
        after = [updated[j + 1][0][0]] if j + 1 < len(updated) else []
        after += [results[j - 2]] if j >= 2 else []
        done.append(
            reduce_columns(
                place_cores, pieces, second_inverse, own_second, other_second, row_count, after
            )
        )
        results.append(lax.all_to_all(done[j], "rows", split_axis=0, concat_axis=0, tiled=True))
        for later in range(AHEAD if j == 1 else j + AHEAD, min(j + AHEAD + 1, chunks) if j else 0):
            update(later)
    turned = jnp.concatenate(results, 1)
    return turned.reshape(row_count * piece, narrow)


def solution(mesh):
    return jax.shard_map(
        on_device,
        mesh=mesh,
        in_specs=(P("rows", "cols"), P(), P(None, "cols", "rows"), P(), P(None, "cols", "rows")),
        out_specs=P("cols", "rows"),
        check_vma=False,
    )
```

```python
import functools

import jax
import jax.numpy as jnp
from jax import lax
from jax.experimental import pallas as pl
from jax.experimental.pallas import tpu as pltpu
from jax.sharding import PartitionSpec as P

BLOCK = 128
AHEAD = 2
SHARE = 1000
PLAIN = (((1,), (0,)), ((), ()))
CONTRACT_COLS = (((1,), (1,)), ((), ()))
ANY = pl.BlockSpec(memory_space=pl.ANY)


def split(value):
    high = value.astype(jnp.bfloat16)
    low = (value - high.astype(jnp.float32)).astype(jnp.bfloat16)
    return high, low


def product(left, right, contract=PLAIN):
    def one(a, b):
        return lax.dot_general(a, b, contract, preferred_element_type=jnp.float32)

    return one(left[0], right[0]) + (one(left[0], right[1]) + one(left[1], right[0]))


def whole(shape):
    return pl.BlockSpec(shape, lambda *_: (0,) * len(shape))


def cost(flops, read):
    return pl.CostEstimate(flops=flops // SHARE, bytes_accessed=read // SHARE, transcendentals=0)


def compiler_params(mib):
    return pltpu.CompilerParams(vmem_limit_bytes=mib * 2**20)


def solve_kernel(panels, place, own, other, inverse_ref, corner_ref, *refs):
    solved_ref, high_ref, low_ref, head, inv_high, inv_low, cor_high, cor_low = refs
    width = inverse_ref.shape[1]
    blocks = width // BLOCK

    @pl.when(pl.program_id(0) == 0)
    def _():
        for k in range(panels):
            inv_high[k], inv_low[k] = split(inverse_ref[k])
            for p in range(k):
                for b in range(blocks):
                    rows = slice((k * blocks + b) * BLOCK, (k * blocks + b + 1) * BLOCK)
                    for c in range(corner_ref.shape[0]):
                        parts = split(corner_ref[c, (k - 1) * blocks + b, p].T)
                        held = corner_ref.shape[3]
                        columns = slice(c * held, (c + 1) * held)
                        cor_high[p, rows, columns], cor_low[p, rows, columns] = parts

    for b in range(panels * blocks):
        mine = jnp.where(place[0] == b % 2, own[b // 2], other[b // 2])
        head[b * BLOCK : (b + 1) * BLOCK] = mine
    parts = []
    for k in range(panels):
        rows = slice(k * width, (k + 1) * width)
        current = head[rows]
        for p in range(k):
            block = (cor_high[p, rows], cor_low[p, rows])
            current = current - product(block, parts[p])
        answer = product((inv_high[k], inv_low[k]), split(current))
        parts.append(split(answer))
        solved_ref[rows] = answer
        high_ref[rows] = parts[k][0]
        low_ref[rows] = parts[k][1]


def solve_rows(place, own, other, inverse, corner):
    panels, width, _ = inverse.shape
    breadth = own.shape[2]
    depth = panels * width
    tile = min(breadth, 256)
    half = pl.BlockSpec((depth // BLOCK // 2, BLOCK, tile), lambda i, _: (0, 0, i))
    block = pl.BlockSpec((depth, tile), lambda i, _: (0, i))
    corner_shape = (panels - 1, depth, width)
    return pl.pallas_call(
        functools.partial(solve_kernel, panels),
        grid_spec=pltpu.PrefetchScalarGridSpec(
            num_scalar_prefetch=1,
            grid=(breadth // tile,),
            in_specs=[half, half, whole(inverse.shape), whole(corner.shape)],
            out_specs=[block] * 3,
            scratch_shapes=[
                pltpu.VMEM((depth, tile), jnp.float32),
                pltpu.VMEM(inverse.shape, jnp.bfloat16),
                pltpu.VMEM(inverse.shape, jnp.bfloat16),
                pltpu.VMEM(corner_shape, jnp.bfloat16),
                pltpu.VMEM(corner_shape, jnp.bfloat16),
            ],
        ),
        out_shape=[
            jax.ShapeDtypeStruct((depth, breadth), t)
            for t in (jnp.float32, jnp.bfloat16, jnp.bfloat16)
        ],
        compiler_params=compiler_params(60),
        cost_estimate=cost(6 * 3 * width * width * breadth, 16 * depth * breadth),
        name="solve_rows",
    )(place, own, other, inverse, corner)


def update_kernel(tops, slots, offset, count, place, slab, *rest):
    factors = rest[:count]
    high, low, own_top = rest[count : count + 3]
    outs = rest[-slots - 3 : -3]
    factor_high, factor_low, total = rest[-3:]

    @pl.when(pl.program_id(0) == 0)
    def _():
        panels, share, columns = factors[0].shape
        held = columns // slots
        chunk = slab.shape[1]
        for dest in range(slots):
            rows = slice(dest * chunk, (dest + 1) * chunk)
            taken = slice(dest * held + offset, dest * held + offset + chunk)
            for panel in range(panels):
                for slot in range(count):
                    start = pl.multiple_of((place[1] ^ slot) * share, BLOCK)
                    at = pl.ds(panel * share * count + start, share)
                    parts = split(factors[slot][panel, :, taken].T)
                    factor_high[rows, at], factor_low[rows, at] = parts

    answer = product((factor_high[...], factor_low[...]), (high[...], low[...]))
    total[...] = answer.reshape(total.shape)
    for dest, first, count, flag in tops:

        @pl.when(place[2 + flag] > 0)
        def _():
            total[dest, :count] = slab[dest, :count] - own_top[first : first + count]

    for slot in range(slots):
        dest = place[0] ^ slot
        outs[slot][...] = slab[dest] - total[dest]


def update_rows(place, slab, factors, high, low, own_top, begin, chunk, offset, after):
    slots, piece, breadth = slab.shape
    depth = high.shape[0]
    tile = min(breadth, 256)
    assert begin % chunk == 0
    tops = []
    for dest in range(slots):
        first = dest * piece + begin
        for b in range(own_top.shape[0] // BLOCK):
            start, stop = max(first, b * BLOCK), min(first + chunk, (b + 1) * BLOCK)
            if start < stop:
                assert start == first
                tops.append((dest, start, stop - start, b))
    columns = pl.BlockSpec((depth, tile), lambda i, _: (0, i))
    return pl.pallas_call(
        functools.partial(update_kernel, tops, slots, offset, len(factors)),
        grid_spec=pltpu.PrefetchScalarGridSpec(
            num_scalar_prefetch=1,
            grid=(breadth // tile,),
            in_specs=[
                pl.BlockSpec((slots, chunk, tile), lambda i, _: (0, begin // chunk, i)),
                *[whole(f.shape) for f in factors],
                columns,
                columns,
                pl.BlockSpec((own_top.shape[0], tile), lambda i, _: (0, i)),
            ]
            + [ANY] * len(after),
            out_specs=[pl.BlockSpec((chunk, tile), lambda i, _: (0, i))] * slots,
            scratch_shapes=[
                pltpu.VMEM((slots * chunk, depth), jnp.bfloat16),
                pltpu.VMEM((slots * chunk, depth), jnp.bfloat16),
                pltpu.VMEM((slots, chunk, tile), jnp.float32),
            ],
        ),
        out_shape=[jax.ShapeDtypeStruct((chunk, breadth), jnp.float32)] * slots,
        compiler_params=compiler_params(60),
        cost_estimate=cost(12 * slots * chunk * depth * breadth, 12 * depth * breadth),
        name="update_rows",
    )(place, slab, *factors, high, low, own_top, *after)


def reduce_kernel(slots, views, extra, place, *refs):
    pieces = refs[:slots]
    inverse = refs[slots]
    own = refs[slots + 1 : slots + 1 + views]
    other = refs[slots + 1 + views : slots + 1 + 2 * views]
    out, current, high, low, factor_high, factor_low = refs[slots + 1 + 2 * views + extra :]
    step = pl.program_id(0)
    chunk, breadth = pieces[0].shape
    width = inverse.shape[1]
    depth = current.shape[1]
    narrow = out.shape[2]
    span = depth // breadth
    count, _, piece, _ = own[0].shape
    core = place[1]

    for part in range(span):
        for slot in range(slots):

            @pl.when((step * span + part) ^ place[0] == slot)
            def _():
                current[:, part * breadth : (part + 1) * breadth] = pieces[slot][...]

    def load(group, panels):
        for parity in range(2):
            sources = own if parity == group % 2 else other

            @pl.when(core == parity)
            def _():
                for panel in range(panels):
                    for part in range(count):
                        start = panel * width + part * piece
                        rows = slice(start, start + piece)
                        parts = split(sources[group // 2 * 2 + panel][part, 0])
                        factor_high[rows], factor_low[rows] = parts

    def store(value, start):
        for g in range(value.shape[1] // narrow):
            out[start // narrow + g] = value[:, g * narrow : (g + 1) * narrow]

    @pl.when(step == 0)
    def _():
        first = product(split(current[:, :width]), split(inverse[0]), CONTRACT_COLS)
        first_parts = split(first)
        high[:, :width], low[:, :width] = first_parts
        store(first, 0)
        for group in range(width // narrow, depth // narrow):
            load(group, 1)
            columns = slice(group * narrow, (group + 1) * narrow)
            current[:, columns] -= product(first_parts, (factor_high[:width], factor_low[:width]))
        second = product(split(current[:, width:]), split(inverse[1]), CONTRACT_COLS)
        high[:, width:], low[:, width:] = split(second)
        store(second, width)

    @pl.when(step > 0)
    def _():
        for group in range(depth // narrow):
            load(group, 2)
            columns = slice(group * narrow, (group + 1) * narrow)
            part = product((high[...], low[...]), (factor_high[...], factor_low[...]))
            out[group] = current[:, columns] - part


def reduce_columns(place, pieces, inverse, own, other, row_count, after):
    chunk, breadth = pieces[0].shape
    slots = len(pieces)
    panels, width, _ = inverse.shape
    depth = panels * width
    breadth_all = slots * breadth
    narrow = breadth_all // row_count
    span = depth // narrow // 2
    taken = (own.shape[0], 1) + own.shape[2:]

    def view(chip, panel):
        return pl.BlockSpec(
            taken, lambda i, _: (0, jnp.maximum(2 * (span * i + chip) - 1 + panel, 0), 0, 0)
        )

    views = [view(chip, panel) for chip in range(span) for panel in range(2)]
    return pl.pallas_call(
        functools.partial(reduce_kernel, slots, len(views), len(after)),
        grid_spec=pltpu.PrefetchScalarGridSpec(
            num_scalar_prefetch=1,
            grid=(breadth_all // depth,),
            in_specs=[whole(pieces[0].shape)] * slots
            + [whole(inverse.shape)]
            + views * 2
            + [ANY] * len(after),
            out_specs=pl.BlockSpec((depth // narrow, chunk, narrow), lambda i, _: (i, 0, 0)),
            scratch_shapes=[
                pltpu.VMEM((chunk, depth), jnp.float32),
                pltpu.VMEM((chunk, depth), jnp.bfloat16),
                pltpu.VMEM((chunk, depth), jnp.bfloat16),
                pltpu.VMEM((depth, narrow), jnp.bfloat16),
                pltpu.VMEM((depth, narrow), jnp.bfloat16),
            ],
        ),
        out_shape=jax.ShapeDtypeStruct((row_count, chunk, narrow), jnp.float32),
        compiler_params=compiler_params(60),
        cost_estimate=cost(6 * chunk * depth * breadth_all, 4 * depth * breadth_all),
        name="reduce_columns",
    )(place, *pieces, inverse, *[own] * len(views), *[other] * len(views), *after)


def order_kernel(chips, skipped, place, *refs):
    entry = pl.program_id(0)
    for i in range(2 * chips - 1):
        if not skipped:

            @pl.when(entry - place[0] == i - (chips - 1))
            def _():
                refs[-1][0] = refs[i][...]

        else:
            for panel in range(2):
                chip = (entry + 1 - panel) // 2
                held = jnp.logical_and((entry + 1) % 2 == panel, entry > 0)
                first = panel == 0 and entry == 0

                @pl.when(
                    jnp.logical_and(jnp.logical_or(held, first), chip - place[0] == i - (chips - 1))
                )
                def _():
                    refs[-1][0] = refs[i][panel]


def in_order(place, pieces, skipped, after):
    chips = (len(pieces) + 1) // 2
    shape = pieces[0].shape
    entry = shape[1:] if skipped else shape
    count = 2 * chips - 1 if skipped else chips
    return pl.pallas_call(
        functools.partial(order_kernel, chips, skipped),
        grid_spec=pltpu.PrefetchScalarGridSpec(
            num_scalar_prefetch=1,
            grid=(count,),
            in_specs=[whole(shape)] * len(pieces) + [ANY] * len(after),
            out_specs=pl.BlockSpec((1,) + entry, lambda i, _: (i,) + (0,) * len(entry)),
        ),
        out_shape=jax.ShapeDtypeStruct((count,) + entry, jnp.float32),
        compiler_params=compiler_params(60),
        name="in_order",
    )(place, *pieces, *after)


def along_line(block, row_count, skipped, after):
    chips = row_count // 2
    up = [(i, i + 2) for i in range(row_count - 2)]
    down = [(i + 2, i) for i in range(row_count - 2)]
    below, above = [block], [block]
    for _ in range(chips - 1):
        below.append(lax.ppermute(below[-1], "rows", up))
        above.append(lax.ppermute(above[-1], "rows", down))
    place = jnp.stack([lax.axis_index("rows") // 2])
    return in_order(place, below[:0:-1] + above, skipped, after), [below[-1], above[-1]]


def gate_kernel(*refs):
    pass


def gate(value, after):
    return pl.pallas_call(
        gate_kernel,
        in_specs=[ANY] * (1 + len(after)),
        out_specs=ANY,
        out_shape=jax.ShapeDtypeStruct(value.shape, value.dtype),
        input_output_aliases={0: 0},
        compiler_params=compiler_params(60),
        name="gate",
    )(value, *after)


def pick_kernel(axis, count, *refs):
    out = refs[-1]
    extent = out.shape[axis] // count
    for i in range(count):
        at = (slice(None),) * axis + (slice(i * extent, (i + 1) * extent),)
        out[at] = refs[i][...]


def pick_blocks(source, axis, extent, blocks, after):
    ndim = source.ndim

    def sized(size):
        return source.shape[:axis] + (size,) + source.shape[axis + 1 :]

    def spec(place):
        return pl.BlockSpec(sized(extent), lambda _: (0,) * axis + (place,) + (0,) * (ndim - axis - 1))

    result = sized(extent * len(blocks))
    return pl.pallas_call(
        functools.partial(pick_kernel, axis, len(blocks)),
        grid=(1,),
        in_specs=[spec(b) for b in blocks] + [ANY] * len(after),
        out_specs=whole(result),
        out_shape=jax.ShapeDtypeStruct(result, source.dtype),
        compiler_params=compiler_params(60),
        name="pick_blocks",
    )(*[source] * len(blocks), *after)


def on_device(window_slab, first_inverse, first_factor, second_inverse, second_factor):
    row_count = lax.axis_size("rows")
    col_count = lax.axis_size("cols")
    row_index = lax.axis_index("rows")
    col_index = lax.axis_index("cols")
    core = row_index % 2
    row_share, breadth = window_slab.shape
    panels, width, _ = first_inverse.shape
    depth = panels * width
    assert depth <= row_count * BLOCK and panels == 2
    piece = row_share // col_count
    if piece == 6 * BLOCK:
        sizes, groups = [BLOCK] * 6, [[0, 1], [2, 3], [4, 5]]
    else:
        sizes, groups = [piece], [[0]]
    begins = [sum(sizes[:j]) for j in range(len(sizes))]
    chunks = len(sizes)
    narrow = breadth * col_count // row_count
    swap = [(i, i ^ 1) for i in range(row_count)]

    def from_sibling(value):
        return lax.ppermute(value, "rows", swap)

    over_cols = [[(i, i ^ s) for i in range(col_count)] for s in range(col_count)]

    def gather_factor(group, after):
        begin, extent = begins[group[0]], sum(sizes[j] for j in group)
        if piece % BLOCK == 0:
            blocks = [(d * piece + begin) // extent for d in range(col_count)]
            part = pick_blocks(first_factor, 2, extent, blocks, after)
        else:
            columns = [d * piece + begin for d in range(col_count)]
            part = jnp.concatenate([first_factor[:, :, c : c + extent] for c in columns], 2)
        return [lax.all_gather(part, "cols", axis=1, tiled=True)]

    factors = [gather_factor(groups[0], [])]

    line, last = along_line(second_factor, row_count, True, factors[0])
    own_second = lax.all_gather(line, "cols")

    corner = pick_blocks(first_factor[: panels - 1, :, :BLOCK], 2, BLOCK, [0], [line])
    corner = lax.all_gather(corner, "rows")[width // BLOCK : depth // BLOCK]
    if col_count == 4:
        corner = jnp.stack([corner] + [lax.ppermute(corner, "cols", p) for p in over_cols[1:]])
        corner = corner[jnp.arange(col_count) ^ col_index]
    else:
        corner = lax.all_gather(corner, "cols")

    own_head, _ = along_line(pick_blocks(window_slab, 0, BLOCK, [0], [line]), row_count, False, [corner])
    other_head = from_sibling(own_head)
    solved, solved_high, solved_low = solve_rows(
        jnp.stack([core]), own_head, other_head, first_inverse, corner
    )
    start = row_index * BLOCK
    own_top = lax.dynamic_slice_in_dim(solved, jnp.minimum(start, depth - BLOCK), BLOCK, 0)
    is_top = (start < depth).astype(jnp.int32)

    slab = window_slab.reshape(col_count, piece, breadth)
    updated, done, results, ready = [], [], [], []

    def update(j):
        number = next(g for g, group in enumerate(groups) if j in group)
        after = [done[j - AHEAD]] if j >= AHEAD else ready
        out = update_rows(
            jnp.stack([col_index, jnp.int32(0), is_top]),
            slab,
            factors[number],
            solved_high,
            solved_low,
            own_top,
            begins[j],
            sizes[j],
            begins[j] - begins[groups[number][0]],
            after,
        )
        pieces = [out[0]]
        for slot in range(1, col_count):
            pieces.append(lax.ppermute(out[slot], "cols", over_cols[slot]))
        updated.append((out, pieces))

    update(0)

    own_second = gate(own_second, [updated[0][0][0]])
    other_second = from_sibling(own_second)
    place_cores = jnp.stack([col_index, core])
    ready = [own_second]
    if chunks > 1:
        update(1)
    factors += [gather_factor(group, ready) for group in groups[1:]]

    for j in range(chunks):
        pieces = updated[j][1]
        after = [updated[j + 1][0][0]] if j + 1 < len(updated) else []
        after += [results[j - 2]] if j >= 2 else []
        done.append(
            reduce_columns(
                place_cores, pieces, second_inverse, own_second, other_second, row_count, after
            )
        )
        results.append(lax.all_to_all(done[j], "rows", split_axis=0, concat_axis=0, tiled=True))
        if j + AHEAD < chunks:
            update(j + AHEAD)
    turned = jnp.concatenate(results, 1)
    return turned.reshape(row_count * piece, narrow)


def solution(mesh):
    return jax.shard_map(
        on_device,
        mesh=mesh,
        in_specs=(P("rows", "cols"), P(), P(None, "cols", "rows"), P(), P(None, "cols", "rows")),
        out_specs=P("cols", "rows"),
        check_vma=False,
    )
```

```python
import functools

import jax
import jax.numpy as jnp
from jax import lax
from jax.experimental import pallas as pl
from jax.experimental.pallas import tpu as pltpu
from jax.sharding import PartitionSpec as P

BLOCK = 128
AHEAD = 2
SHARE = 1000
PLAIN = (((1,), (0,)), ((), ()))
CONTRACT_COLS = (((1,), (1,)), ((), ()))
ANY = pl.BlockSpec(memory_space=pl.ANY)


def split(value):
    high = value.astype(jnp.bfloat16)
    low = (value - high.astype(jnp.float32)).astype(jnp.bfloat16)
    return high, low


def product(left, right, contract=PLAIN):
    def one(a, b):
        return lax.dot_general(a, b, contract, preferred_element_type=jnp.float32)

    return one(left[0], right[0]) + (one(left[0], right[1]) + one(left[1], right[0]))


def stacked_product(both, high, low):
    rows = both.shape[0] // 2
    first = jnp.dot(both[...], high, preferred_element_type=jnp.float32)
    second = jnp.dot(both[:rows], low, preferred_element_type=jnp.float32)
    return first[:rows] + (first[rows:] + second)


def whole(shape):
    return pl.BlockSpec(shape, lambda *_: (0,) * len(shape))


def cost(flops, read):
    return pl.CostEstimate(flops=flops // SHARE, bytes_accessed=read // SHARE, transcendentals=0)


def compiler_params(mib):
    return pltpu.CompilerParams(vmem_limit_bytes=mib * 2**20)


def solve_kernel(panels, place, own, other, inverse_ref, corner_ref, *refs):
    solved_ref, high_ref, low_ref, head, inv_high, inv_low, cor_high, cor_low = refs
    width = inverse_ref.shape[1]
    blocks = width // BLOCK

    @pl.when(pl.program_id(0) == 0)
    def _():
        for k in range(panels):
            inv_high[k], inv_low[k] = split(inverse_ref[k])
            for p in range(k):
                for b in range(blocks):
                    rows = slice((k * blocks + b) * BLOCK, (k * blocks + b + 1) * BLOCK)
                    for c in range(corner_ref.shape[0]):
                        parts = split(corner_ref[c, (k - 1) * blocks + b, p].T)
                        held = corner_ref.shape[3]
                        columns = slice(c * held, (c + 1) * held)
                        cor_high[p, rows, columns], cor_low[p, rows, columns] = parts

    for b in range(panels * blocks):
        mine = jnp.where(place[0] == b % 2, own[b // 2], other[b // 2])
        head[b * BLOCK : (b + 1) * BLOCK] = mine
    parts = []
    for k in range(panels):
        rows = slice(k * width, (k + 1) * width)
        current = head[rows]
        for p in range(k):
            block = (cor_high[p, rows], cor_low[p, rows])
            current = current - product(block, parts[p])
        half = width // 2
        known = split(current)
        upper = product(
            (inv_high[k, :half, :half], inv_low[k, :half, :half]),
            (known[0][:half], known[1][:half]),
        )
        lower = product((inv_high[k, half:], inv_low[k, half:]), known)
        answer = jnp.concatenate([upper, lower], 0)
        parts.append(split(answer))
        solved_ref[rows] = answer
        high_ref[rows] = parts[k][0]
        low_ref[rows] = parts[k][1]


def solve_rows(place, own, other, inverse, corner):
    panels, width, _ = inverse.shape
    breadth = own.shape[2]
    depth = panels * width
    tile = min(breadth, 256)
    half = pl.BlockSpec((depth // BLOCK // 2, BLOCK, tile), lambda i, _: (0, 0, i))
    block = pl.BlockSpec((depth, tile), lambda i, _: (0, i))
    corner_shape = (panels - 1, depth, width)
    return pl.pallas_call(
        functools.partial(solve_kernel, panels),
        grid_spec=pltpu.PrefetchScalarGridSpec(
            num_scalar_prefetch=1,
            grid=(breadth // tile,),
            in_specs=[half, half, whole(inverse.shape), whole(corner.shape)],
            out_specs=[block] * 3,
            scratch_shapes=[
                pltpu.VMEM((depth, tile), jnp.float32),
                pltpu.VMEM(inverse.shape, jnp.bfloat16),
                pltpu.VMEM(inverse.shape, jnp.bfloat16),
                pltpu.VMEM(corner_shape, jnp.bfloat16),
                pltpu.VMEM(corner_shape, jnp.bfloat16),
            ],
        ),
        out_shape=[
            jax.ShapeDtypeStruct((depth, breadth), t)
            for t in (jnp.float32, jnp.bfloat16, jnp.bfloat16)
        ],
        compiler_params=compiler_params(60),
        cost_estimate=cost(6 * 3 * width * width * breadth, 16 * depth * breadth),
        name="solve_rows",
    )(place, own, other, inverse, corner)


def update_kernel(tops, slots, offset, place, slab, factor, high, low, own_top, *rest):
    outs = rest[-slots - 2 : -2]
    both, total = rest[-2:]
    rows = both.shape[0] // 2
    chunk = rows // slots

    @pl.when(pl.program_id(0) == 0)
    def _():
        held = factor.shape[1] // slots
        for dest in range(slots):
            at = dest * chunk
            taken = slice(dest * held + offset, dest * held + offset + chunk)
            both[at : at + chunk], both[rows + at : rows + at + chunk] = split(factor[:, taken].T)

    total[...] = stacked_product(both, high[...], low[...]).reshape(total.shape)
    for dest, first, count in tops:

        @pl.when(place[2] > 0)
        def _():
            total[dest, :count] = slab[dest, :count] - own_top[first : first + count]

    for slot in range(slots):
        dest = place[0] ^ slot
        outs[slot][...] = slab[dest] - total[dest]


def update_rows(place, slab, factor, high, low, solved, begin, chunk, offset, after):
    slots, piece, breadth = slab.shape
    depth = high.shape[0]
    tile = min(breadth, 256)
    assert begin % chunk == 0
    tops = []
    for dest in range(slots):
        first = dest * piece + begin
        if first < BLOCK:
            tops.append((dest, first, min(chunk, BLOCK - first)))
    columns = pl.BlockSpec((depth, tile), lambda i, _: (0, i))
    return pl.pallas_call(
        functools.partial(update_kernel, tops, slots, offset),
        grid_spec=pltpu.PrefetchScalarGridSpec(
            num_scalar_prefetch=1,
            grid=(breadth // tile,),
            in_specs=[
                pl.BlockSpec((slots, chunk, tile), lambda i, _: (0, begin // chunk, i)),
                whole(factor.shape),
                columns,
                columns,
                pl.BlockSpec((BLOCK, tile), lambda i, place: (place[1], i)),
            ]
            + [ANY] * len(after),
            out_specs=[pl.BlockSpec((chunk, tile), lambda i, _: (0, i))] * slots,
            scratch_shapes=[
                pltpu.VMEM((2 * slots * chunk, depth), jnp.bfloat16),
                pltpu.VMEM((slots, chunk, tile), jnp.float32),
            ],
        ),
        out_shape=[jax.ShapeDtypeStruct((chunk, breadth), jnp.float32)] * slots,
        compiler_params=compiler_params(60),
        cost_estimate=cost(12 * slots * chunk * depth * breadth, 12 * depth * breadth),
        name="update_rows",
    )(place, slab, factor, high, low, solved, *after)


def reduce_kernel(slots, views, extra, place, *refs):
    pieces = refs[:slots]
    inverse = refs[slots]
    own = refs[slots + 1 : slots + 1 + views]
    other = refs[slots + 1 + views : slots + 1 + 2 * views]
    out, current, both, factor_high, factor_low = refs[slots + 1 + 2 * views + extra :]
    step = pl.program_id(0)
    chunk, breadth = pieces[0].shape
    width = inverse.shape[1]
    depth = current.shape[1]
    narrow = out.shape[2]
    span = depth // breadth
    count, _, piece, _ = own[0].shape
    core = place[1]

    for part in range(span):
        for slot in range(slots):

            @pl.when((step * span + part) ^ place[0] == slot)
            def _():
                current[:, part * breadth : (part + 1) * breadth] = pieces[slot][...]

    def load(group, panels):
        for parity in range(2):
            sources = own if parity == group % 2 else other

            @pl.when(core == parity)
            def _():
                for panel in range(panels):
                    for part in range(count):
                        start = panel * width + part * piece
                        rows = slice(start, start + piece)
                        parts = split(sources[group // 2 * 2 + panel][part, 0])
                        factor_high[rows], factor_low[rows] = parts

    def store(value, start):
        for g in range(value.shape[1] // narrow):
            out[start // narrow + g] = value[:, g * narrow : (g + 1) * narrow]

    @pl.when(step == 0)
    def _():
        first = product(split(current[:, :width]), split(inverse[0]), CONTRACT_COLS)
        first_parts = split(first)
        both[:chunk, :width], both[chunk:, :width] = first_parts
        store(first, 0)
        for group in range(width // narrow, depth // narrow):
            load(group, 1)
            columns = slice(group * narrow, (group + 1) * narrow)
            current[:, columns] -= product(first_parts, (factor_high[:width], factor_low[:width]))
        second = product(split(current[:, width:]), split(inverse[1]), CONTRACT_COLS)
        both[:chunk, width:], both[chunk:, width:] = split(second)
        store(second, width)

    @pl.when(step > 0)
    def _():
        for group in range(depth // narrow):
            load(group, 2)
            columns = slice(group * narrow, (group + 1) * narrow)
            part = stacked_product(both, factor_high[...], factor_low[...])
            out[group] = current[:, columns] - part


def reduce_columns(place, pieces, inverse, own, other, row_count, after):
    chunk, breadth = pieces[0].shape
    slots = len(pieces)
    panels, width, _ = inverse.shape
    depth = panels * width
    breadth_all = slots * breadth
    narrow = breadth_all // row_count
    span = depth // narrow // 2
    taken = (own.shape[0], 1) + own.shape[2:]

    def view(chip, panel):
        return pl.BlockSpec(
            taken, lambda i, _: (0, jnp.maximum(2 * (span * i + chip) - 1 + panel, 0), 0, 0)
        )

    views = [view(chip, panel) for chip in range(span) for panel in range(2)]
    return pl.pallas_call(
        functools.partial(reduce_kernel, slots, len(views), len(after)),
        grid_spec=pltpu.PrefetchScalarGridSpec(
            num_scalar_prefetch=1,
            grid=(breadth_all // depth,),
            in_specs=[whole(pieces[0].shape)] * slots
            + [whole(inverse.shape)]
            + views * 2
            + [ANY] * len(after),
            out_specs=pl.BlockSpec((depth // narrow, chunk, narrow), lambda i, _: (i, 0, 0)),
            scratch_shapes=[
                pltpu.VMEM((chunk, depth), jnp.float32),
                pltpu.VMEM((2 * chunk, depth), jnp.bfloat16),
                pltpu.VMEM((depth, narrow), jnp.bfloat16),
                pltpu.VMEM((depth, narrow), jnp.bfloat16),
            ],
        ),
        out_shape=jax.ShapeDtypeStruct((row_count, chunk, narrow), jnp.float32),
        compiler_params=compiler_params(60),
        cost_estimate=cost(6 * chunk * depth * breadth_all, 4 * depth * breadth_all),
        name="reduce_columns",
    )(place, *pieces, inverse, *[own] * len(views), *[other] * len(views), *after)


def order_kernel(chips, skipped, place, *refs):
    entry = pl.program_id(0)
    for i in range(2 * chips - 1):
        if not skipped:

            @pl.when(entry - place[0] == i - (chips - 1))
            def _():
                refs[-1][0] = refs[i][...]

        else:
            for panel in range(2):
                chip = (entry + 1 - panel) // 2
                held = jnp.logical_and((entry + 1) % 2 == panel, entry > 0)
                first = panel == 0 and entry == 0

                @pl.when(
                    jnp.logical_and(jnp.logical_or(held, first), chip - place[0] == i - (chips - 1))
                )
                def _():
                    refs[-1][0] = refs[i][panel]


def in_order(place, pieces, skipped, after):
    chips = (len(pieces) + 1) // 2
    shape = pieces[0].shape
    entry = shape[1:] if skipped else shape
    count = 2 * chips - 1 if skipped else chips
    return pl.pallas_call(
        functools.partial(order_kernel, chips, skipped),
        grid_spec=pltpu.PrefetchScalarGridSpec(
            num_scalar_prefetch=1,
            grid=(count,),
            in_specs=[whole(shape)] * len(pieces) + [ANY] * len(after),
            out_specs=pl.BlockSpec((1,) + entry, lambda i, _: (i,) + (0,) * len(entry)),
        ),
        out_shape=jax.ShapeDtypeStruct((count,) + entry, jnp.float32),
        compiler_params=compiler_params(60),
        name="in_order",
    )(place, *pieces, *after)


def along_lines(blocks, row_count):
    chips = row_count // 2
    up = [(i, i + 2) for i in range(row_count - 2)]
    down = [(i + 2, i) for i in range(row_count - 2)]
    below, above = [[b] for b in blocks], [[b] for b in blocks]
    for step in range(chips - 1):
        for n in range(len(blocks)):
            below[n].append(lax.ppermute(below[n][-1], "rows", up))
            above[n].append(lax.ppermute(above[n][-1], "rows", down))
        if step < chips - 2:
            brought = [side[n][-1] for n in range(1, len(blocks)) for side in (below, above)]
            below[0][-1] = gate(below[0][-1], brought)
            above[0][-1] = gate(above[0][-1], brought)
    return [below[n][:0:-1] + above[n] for n in range(len(blocks))]


def gate_kernel(*refs):
    pass


def gate(value, after):
    return pl.pallas_call(
        gate_kernel,
        in_specs=[ANY] * (1 + len(after)),
        out_specs=ANY,
        out_shape=jax.ShapeDtypeStruct(value.shape, value.dtype),
        input_output_aliases={0: 0},
        compiler_params=compiler_params(60),
        name="gate",
    )(value, *after)


def pick_kernel(axis, count, *refs):
    out = refs[-1]
    extent = out.shape[axis] // count
    for i in range(count):
        at = (slice(None),) * axis + (slice(i * extent, (i + 1) * extent),)
        out[at] = refs[i][...]


def pick_blocks(source, axis, extent, blocks, after):
    ndim = source.ndim

    def sized(size):
        return source.shape[:axis] + (size,) + source.shape[axis + 1 :]

    def spec(place):
        return pl.BlockSpec(sized(extent), lambda _: (0,) * axis + (place,) + (0,) * (ndim - axis - 1))

    result = sized(extent * len(blocks))
    return pl.pallas_call(
        functools.partial(pick_kernel, axis, len(blocks)),
        grid=(1,),
        in_specs=[spec(b) for b in blocks] + [ANY] * len(after),
        out_specs=whole(result),
        out_shape=jax.ShapeDtypeStruct(result, source.dtype),
        compiler_params=compiler_params(60),
        name="pick_blocks",
    )(*[source] * len(blocks), *after)


def on_device(window_slab, first_inverse, first_factor, second_inverse, second_factor):
    row_count = lax.axis_size("rows")
    col_count = lax.axis_size("cols")
    row_index = lax.axis_index("rows")
    col_index = lax.axis_index("cols")
    core = row_index % 2
    row_share, breadth = window_slab.shape
    panels, width, _ = first_inverse.shape
    depth = panels * width
    assert depth <= row_count * BLOCK and panels == 2
    piece = row_share // col_count
    if piece == 6 * BLOCK:
        sizes, groups = [BLOCK] * 6, [[0, 1], [2, 3], [4, 5]]
    else:
        sizes, groups = [piece], [[0]]
    begins = [sum(sizes[:j]) for j in range(len(sizes))]
    chunks = len(sizes)
    narrow = breadth * col_count // row_count
    swap = [(i, i ^ 1) for i in range(row_count)]

    def from_sibling(value):
        return lax.ppermute(value, "rows", swap)

    over_cols = [[(i, i ^ s) for i in range(col_count)] for s in range(col_count)]

    def gather_factor(group, after):
        begin, extent = begins[group[0]], sum(sizes[j] for j in group)
        if piece % BLOCK == 0:
            blocks = [(d * piece + begin) // extent for d in range(col_count)]
            part = pick_blocks(first_factor, 2, extent, blocks, after)
        else:
            columns = [d * piece + begin for d in range(col_count)]
            part = jnp.concatenate([first_factor[:, :, c : c + extent] for c in columns], 2)
        part = lax.all_gather(part, "cols", axis=1, tiled=True)
        return part.reshape(depth, -1)

    factors = [gather_factor(groups[0], [])]

    second_line, head_line = along_lines([second_factor, window_slab[:BLOCK]], row_count)
    chip = jnp.stack([row_index // 2])

    line = in_order(chip, second_line, True, [factors[0]])
    own_second = lax.all_gather(line, "cols")

    corner = pick_blocks(first_factor[: panels - 1, :, :BLOCK], 2, BLOCK, [0], second_line[-2:-1])
    corner = lax.all_gather(corner, "rows")[width // BLOCK : depth // BLOCK]
    own_head = in_order(chip, head_line, False, [corner])
    other_head = from_sibling(own_head)
    if col_count == 4:
        corner = jnp.stack([corner] + [lax.ppermute(corner, "cols", p) for p in over_cols[1:]])
        corner = corner[jnp.arange(col_count) ^ col_index]
    else:
        corner = lax.all_gather(corner, "cols")

    solved, solved_high, solved_low = solve_rows(
        jnp.stack([core]), own_head, other_head, first_inverse, corner
    )
    is_top = (row_index * BLOCK < depth).astype(jnp.int32)
    own_block = jnp.minimum(row_index, depth // BLOCK - 1)

    slab = window_slab.reshape(col_count, piece, breadth)
    updated, done, results, ready = [], [], [], []

    def update(j):
        number = next(g for g, group in enumerate(groups) if j in group)
        after = [done[j - AHEAD]] if j >= AHEAD else ready
        out = update_rows(
            jnp.stack([col_index, own_block, is_top]),
            slab,
            factors[number],
            solved_high,
            solved_low,
            solved,
            begins[j],
            sizes[j],
            begins[j] - begins[groups[number][0]],
            after,
        )
        pieces = [out[0]]
        for slot in range(1, col_count):
            pieces.append(lax.ppermute(out[slot], "cols", over_cols[slot]))
        updated.append((out, pieces))

    update(0)

    own_second = gate(own_second, [updated[0][0][0]])
    other_second = from_sibling(own_second)
    place_cores = jnp.stack([col_index, core])
    ready = [own_second]
    if chunks > 1:
        update(1)
    factors += [gather_factor(group, ready) for group in groups[1:]]

    for j in range(chunks):
        pieces = updated[j][1]
        after = [updated[j + 1][0][0]] if j + 1 < len(updated) else []
        after += [results[j - 2]] if j >= 2 else []
        done.append(
            reduce_columns(
                place_cores, pieces, second_inverse, own_second, other_second, row_count, after
            )
        )
        results.append(lax.all_to_all(done[j], "rows", split_axis=0, concat_axis=0, tiled=True))
        if j + AHEAD < chunks:
            update(j + AHEAD)
    turned = jnp.concatenate(results, 1)
    return turned.reshape(row_count * piece, narrow)


def solution(mesh):
    return jax.shard_map(
        on_device,
        mesh=mesh,
        in_specs=(P("rows", "cols"), P(), P(None, "cols", "rows"), P(), P(None, "cols", "rows")),
        out_specs=P("cols", "rows"),
        check_vma=False,
    )
```

```python
import functools

import jax
import jax.numpy as jnp
from jax import lax
from jax.experimental import pallas as pl
from jax.experimental.pallas import tpu as pltpu
from jax.sharding import PartitionSpec as P

BLOCK = 128
AHEAD = 2
SHARE = 1000
PLAIN = (((1,), (0,)), ((), ()))
CONTRACT_COLS = (((1,), (1,)), ((), ()))
ANY = pl.BlockSpec(memory_space=pl.ANY)


def split(value):
    high = value.astype(jnp.bfloat16)
    low = (value - high.astype(jnp.float32)).astype(jnp.bfloat16)
    return high, low


def product(left, right, contract=PLAIN):
    def one(a, b):
        return lax.dot_general(a, b, contract, preferred_element_type=jnp.float32)

    return one(left[0], right[0]) + (one(left[0], right[1]) + one(left[1], right[0]))


def stacked_product(both, high, low):
    rows = both.shape[0] // 2
    first = jnp.dot(both[...], high, preferred_element_type=jnp.float32)
    second = jnp.dot(both[:rows], low, preferred_element_type=jnp.float32)
    return first[:rows] + (first[rows:] + second)


def whole(shape):
    return pl.BlockSpec(shape, lambda *_: (0,) * len(shape))


def cost(flops, read):
    return pl.CostEstimate(flops=flops // SHARE, bytes_accessed=read // SHARE, transcendentals=0)


def compiler_params(mib):
    return pltpu.CompilerParams(vmem_limit_bytes=mib * 2**20)


def solve_kernel(panels, place, own, other, inverse_ref, corner_ref, *refs):
    solved_ref, high_ref, low_ref, head, inv_high, inv_low, cor_high, cor_low = refs
    width = inverse_ref.shape[1]
    blocks = width // BLOCK

    @pl.when(pl.program_id(0) == 0)
    def _():
        for k in range(panels):
            inv_high[k], inv_low[k] = split(inverse_ref[k])
            for p in range(k):
                for b in range(blocks):
                    rows = slice((k * blocks + b) * BLOCK, (k * blocks + b + 1) * BLOCK)
                    for c in range(corner_ref.shape[0]):
                        parts = split(corner_ref[c, (k - 1) * blocks + b, p].T)
                        held = corner_ref.shape[3]
                        columns = slice(c * held, (c + 1) * held)
                        cor_high[p, rows, columns], cor_low[p, rows, columns] = parts

    for b in range(panels * blocks):
        mine = jnp.where(place[0] == b % 2, own[b // 2], other[b // 2])
        head[b * BLOCK : (b + 1) * BLOCK] = mine
    parts = []
    for k in range(panels):
        rows = slice(k * width, (k + 1) * width)
        current = head[rows]
        for p in range(k):
            block = (cor_high[p, rows], cor_low[p, rows])
            current = current - product(block, parts[p])
        half = width // 2
        known = split(current)
        upper = product(
            (inv_high[k, :half, :half], inv_low[k, :half, :half]),
            (known[0][:half], known[1][:half]),
        )
        lower = product((inv_high[k, half:], inv_low[k, half:]), known)
        answer = jnp.concatenate([upper, lower], 0)
        parts.append(split(answer))
        solved_ref[rows] = answer
        high_ref[rows] = parts[k][0]
        low_ref[rows] = parts[k][1]


def solve_rows(place, own, other, inverse, corner):
    panels, width, _ = inverse.shape
    breadth = own.shape[2]
    depth = panels * width
    tile = min(breadth, 256)
    half = pl.BlockSpec((depth // BLOCK // 2, BLOCK, tile), lambda i, _: (0, 0, i))
    block = pl.BlockSpec((depth, tile), lambda i, _: (0, i))
    corner_shape = (panels - 1, depth, width)
    return pl.pallas_call(
        functools.partial(solve_kernel, panels),
        grid_spec=pltpu.PrefetchScalarGridSpec(
            num_scalar_prefetch=1,
            grid=(breadth // tile,),
            in_specs=[half, half, whole(inverse.shape), whole(corner.shape)],
            out_specs=[block] * 3,
            scratch_shapes=[
                pltpu.VMEM((depth, tile), jnp.float32),
                pltpu.VMEM(inverse.shape, jnp.bfloat16),
                pltpu.VMEM(inverse.shape, jnp.bfloat16),
                pltpu.VMEM(corner_shape, jnp.bfloat16),
                pltpu.VMEM(corner_shape, jnp.bfloat16),
            ],
        ),
        out_shape=[
            jax.ShapeDtypeStruct((depth, breadth), t)
            for t in (jnp.float32, jnp.bfloat16, jnp.bfloat16)
        ],
        compiler_params=compiler_params(60),
        cost_estimate=cost(6 * 3 * width * width * breadth, 16 * depth * breadth),
        name="solve_rows",
    )(place, own, other, inverse, corner)


def update_kernel(tops, slots, offset, place, slab, factor, high, low, own_top, *rest):
    outs = rest[-slots - 2 : -2]
    both, total = rest[-2:]
    rows = both.shape[0] // 2
    chunk = rows // slots

    @pl.when(pl.program_id(0) == 0)
    def _():
        held = factor.shape[1] // slots
        for dest in range(slots):
            at = dest * chunk
            taken = slice(dest * held + offset, dest * held + offset + chunk)
            both[at : at + chunk], both[rows + at : rows + at + chunk] = split(factor[:, taken].T)

    total[...] = stacked_product(both, high[...], low[...]).reshape(total.shape)
    for dest, first, count in tops:

        @pl.when(place[2] > 0)
        def _():
            total[dest, :count] = slab[dest, :count] - own_top[first : first + count]

    for slot in range(slots):
        dest = place[0] ^ slot
        outs[slot][...] = slab[dest] - total[dest]


def update_rows(place, slab, factor, high, low, solved, begin, chunk, offset, after):
    slots, piece, breadth = slab.shape
    depth = high.shape[0]
    tile = min(breadth, 256)
    assert begin % chunk == 0
    tops = []
    for dest in range(slots):
        first = dest * piece + begin
        if first < BLOCK:
            tops.append((dest, first, min(chunk, BLOCK - first)))
    columns = pl.BlockSpec((depth, tile), lambda i, _: (0, i))
    return pl.pallas_call(
        functools.partial(update_kernel, tops, slots, offset),
        grid_spec=pltpu.PrefetchScalarGridSpec(
            num_scalar_prefetch=1,
            grid=(breadth // tile,),
            in_specs=[
                pl.BlockSpec((slots, chunk, tile), lambda i, _: (0, begin // chunk, i)),
                whole(factor.shape),
                columns,
                columns,
                pl.BlockSpec((BLOCK, tile), lambda i, place: (place[1], i)),
            ]
            + [ANY] * len(after),
            out_specs=[pl.BlockSpec((chunk, tile), lambda i, _: (0, i))] * slots,
            scratch_shapes=[
                pltpu.VMEM((2 * slots * chunk, depth), jnp.bfloat16),
                pltpu.VMEM((slots, chunk, tile), jnp.float32),
            ],
        ),
        out_shape=[jax.ShapeDtypeStruct((chunk, breadth), jnp.float32)] * slots,
        compiler_params=compiler_params(60),
        cost_estimate=cost(12 * slots * chunk * depth * breadth, 12 * depth * breadth),
        name="update_rows",
    )(place, slab, factor, high, low, solved, *after)


def reduce_kernel(slots, views, extra, place, *refs):
    pieces = refs[:slots]
    inverse = refs[slots]
    own = refs[slots + 1 : slots + 1 + views]
    other = refs[slots + 1 + views : slots + 1 + 2 * views]
    out, current, both, factor_high, factor_low = refs[slots + 1 + 2 * views + extra :]
    step = pl.program_id(0)
    chunk, breadth = pieces[0].shape
    width = inverse.shape[1]
    depth = current.shape[1]
    narrow = out.shape[2]
    span = depth // breadth
    count, _, piece, _ = own[0].shape
    core = place[1]

    for part in range(span):
        for slot in range(slots):

            @pl.when((step * span + part) ^ place[0] == slot)
            def _():
                current[:, part * breadth : (part + 1) * breadth] = pieces[slot][...]

    def load(group, panels):
        for parity in range(2):
            sources = own if parity == group % 2 else other

            @pl.when(core == parity)
            def _():
                for panel in range(panels):
                    for part in range(count):
                        start = panel * width + part * piece
                        rows = slice(start, start + piece)
                        parts = split(sources[group // 2 * 2 + panel][part, 0])
                        factor_high[rows], factor_low[rows] = parts

    def store(value, start):
        for g in range(value.shape[1] // narrow):
            out[start // narrow + g] = value[:, g * narrow : (g + 1) * narrow]

    @pl.when(step == 0)
    def _():
        first = product(split(current[:, :width]), split(inverse[0]), CONTRACT_COLS)
        first_parts = split(first)
        both[:chunk, :width], both[chunk:, :width] = first_parts
        store(first, 0)
        for group in range(width // narrow, depth // narrow):
            load(group, 1)
            columns = slice(group * narrow, (group + 1) * narrow)
            current[:, columns] -= product(first_parts, (factor_high[:width], factor_low[:width]))
        second = product(split(current[:, width:]), split(inverse[1]), CONTRACT_COLS)
        both[:chunk, width:], both[chunk:, width:] = split(second)
        store(second, width)

    @pl.when(step > 0)
    def _():
        for group in range(depth // narrow):
            load(group, 2)
            columns = slice(group * narrow, (group + 1) * narrow)
            part = stacked_product(both, factor_high[...], factor_low[...])
            out[group] = current[:, columns] - part


def reduce_columns(place, pieces, inverse, own, other, row_count, after):
    chunk, breadth = pieces[0].shape
    slots = len(pieces)
    panels, width, _ = inverse.shape
    depth = panels * width
    breadth_all = slots * breadth
    narrow = breadth_all // row_count
    span = depth // narrow // 2
    taken = (own.shape[0], 1) + own.shape[2:]

    def view(chip, panel):
        return pl.BlockSpec(
            taken, lambda i, _: (0, jnp.maximum(2 * (span * i + chip) - 1 + panel, 0), 0, 0)
        )

    views = [view(chip, panel) for chip in range(span) for panel in range(2)]
    return pl.pallas_call(
        functools.partial(reduce_kernel, slots, len(views), len(after)),
        grid_spec=pltpu.PrefetchScalarGridSpec(
            num_scalar_prefetch=1,
            grid=(breadth_all // depth,),
            in_specs=[whole(pieces[0].shape)] * slots
            + [whole(inverse.shape)]
            + views * 2
            + [ANY] * len(after),
            out_specs=pl.BlockSpec((depth // narrow, chunk, narrow), lambda i, _: (i, 0, 0)),
            scratch_shapes=[
                pltpu.VMEM((chunk, depth), jnp.float32),
                pltpu.VMEM((2 * chunk, depth), jnp.bfloat16),
                pltpu.VMEM((depth, narrow), jnp.bfloat16),
                pltpu.VMEM((depth, narrow), jnp.bfloat16),
            ],
        ),
        out_shape=jax.ShapeDtypeStruct((row_count, chunk, narrow), jnp.float32),
        compiler_params=compiler_params(60),
        cost_estimate=cost(6 * chunk * depth * breadth_all, 4 * depth * breadth_all),
        name="reduce_columns",
    )(place, *pieces, inverse, *[own] * len(views), *[other] * len(views), *after)


def order_kernel(chips, skipped, place, *refs):
    entry = pl.program_id(0)
    for i in range(2 * chips - 1):
        if not skipped:

            @pl.when(entry - place[0] == i - (chips - 1))
            def _():
                refs[-1][0] = refs[i][...]

        else:
            for panel in range(2):
                chip = (entry + 1 - panel) // 2
                held = jnp.logical_and((entry + 1) % 2 == panel, entry > 0)
                first = panel == 0 and entry == 0

                @pl.when(
                    jnp.logical_and(jnp.logical_or(held, first), chip - place[0] == i - (chips - 1))
                )
                def _():
                    refs[-1][0] = refs[i][panel]


def in_order(place, pieces, skipped, after):
    chips = (len(pieces) + 1) // 2
    shape = pieces[0].shape
    entry = shape[1:] if skipped else shape
    count = 2 * chips - 1 if skipped else chips
    return pl.pallas_call(
        functools.partial(order_kernel, chips, skipped),
        grid_spec=pltpu.PrefetchScalarGridSpec(
            num_scalar_prefetch=1,
            grid=(count,),
            in_specs=[whole(shape)] * len(pieces) + [ANY] * len(after),
            out_specs=pl.BlockSpec((1,) + entry, lambda i, _: (i,) + (0,) * len(entry)),
        ),
        out_shape=jax.ShapeDtypeStruct((count,) + entry, jnp.float32),
        compiler_params=compiler_params(60),
        name="in_order",
    )(place, *pieces, *after)


def along_lines(blocks, row_count):
    chips = row_count // 2
    up = [(i, i + 2) for i in range(row_count - 2)]
    down = [(i + 2, i) for i in range(row_count - 2)]
    below, above = [[b] for b in blocks], [[b] for b in blocks]
    for step in range(chips - 1):
        for n in range(len(blocks)):
            below[n].append(lax.ppermute(below[n][-1], "rows", up))
            above[n].append(lax.ppermute(above[n][-1], "rows", down))
        if step < chips - 2:
            brought = [side[n][-1] for n in range(1, len(blocks)) for side in (below, above)]
            below[0][-1] = gate(below[0][-1], brought)
            above[0][-1] = gate(above[0][-1], brought)
    return [below[n][:0:-1] + above[n] for n in range(len(blocks))]


def gate_kernel(*refs):
    pass


def gate(value, after):
    return pl.pallas_call(
        gate_kernel,
        in_specs=[ANY] * (1 + len(after)),
        out_specs=ANY,
        out_shape=jax.ShapeDtypeStruct(value.shape, value.dtype),
        input_output_aliases={0: 0},
        compiler_params=compiler_params(60),
        name="gate",
    )(value, *after)


def pick_kernel(axis, count, *refs):
    out = refs[-1]
    extent = out.shape[axis] // count
    for i in range(count):
        at = (slice(None),) * axis + (slice(i * extent, (i + 1) * extent),)
        out[at] = refs[i][...]


def pick_blocks(source, axis, extent, blocks, after):
    ndim = source.ndim

    def sized(size):
        return source.shape[:axis] + (size,) + source.shape[axis + 1 :]

    def spec(place):
        return pl.BlockSpec(sized(extent), lambda _: (0,) * axis + (place,) + (0,) * (ndim - axis - 1))

    result = sized(extent * len(blocks))
    return pl.pallas_call(
        functools.partial(pick_kernel, axis, len(blocks)),
        grid=(1,),
        in_specs=[spec(b) for b in blocks] + [ANY] * len(after),
        out_specs=whole(result),
        out_shape=jax.ShapeDtypeStruct(result, source.dtype),
        compiler_params=compiler_params(60),
        name="pick_blocks",
    )(*[source] * len(blocks), *after)


def on_device(window_slab, first_inverse, first_factor, second_inverse, second_factor):
    row_count = lax.axis_size("rows")
    col_count = lax.axis_size("cols")
    row_index = lax.axis_index("rows")
    col_index = lax.axis_index("cols")
    core = row_index % 2
    row_share, breadth = window_slab.shape
    panels, width, _ = first_inverse.shape
    depth = panels * width
    assert depth <= row_count * BLOCK and panels == 2
    piece = row_share // col_count
    if piece == 6 * BLOCK:
        sizes, groups = [BLOCK] * 6, [[0, 1], [2, 3], [4, 5]]
    else:
        sizes, groups = [piece], [[0]]
    begins = [sum(sizes[:j]) for j in range(len(sizes))]
    chunks = len(sizes)
    narrow = breadth * col_count // row_count
    swap = [(i, i ^ 1) for i in range(row_count)]

    def from_sibling(value):
        return lax.ppermute(value, "rows", swap)

    over_cols = [[(i, i ^ s) for i in range(col_count)] for s in range(col_count)]

    def gather_factor(group, after):
        begin, extent = begins[group[0]], sum(sizes[j] for j in group)
        if piece % BLOCK == 0:
            blocks = [(d * piece + begin) // extent for d in range(col_count)]
            part = pick_blocks(first_factor, 2, extent, blocks, after)
        else:
            columns = [d * piece + begin for d in range(col_count)]
            part = jnp.concatenate([first_factor[:, :, c : c + extent] for c in columns], 2)
        part = lax.all_gather(part, "cols", axis=1, tiled=True)
        return part.reshape(depth, -1)

    factors = [gather_factor(groups[0], [])]

    second_line, head_line = along_lines([second_factor, window_slab[:BLOCK]], row_count)
    chip = jnp.stack([row_index // 2])

    line = in_order(chip, second_line, True, [factors[0]])
    own_second = lax.all_gather(line, "cols")

    corner = pick_blocks(first_factor[: panels - 1, :, :BLOCK], 2, BLOCK, [0], second_line[-2:-1])
    corner = lax.all_gather(corner, "rows")[width // BLOCK : depth // BLOCK]
    own_head = in_order(chip, head_line, False, [corner])
    other_head = from_sibling(own_head)
    if col_count == 4:
        corner = jnp.stack([corner] + [lax.ppermute(corner, "cols", p) for p in over_cols[1:]])
        corner = corner[jnp.arange(col_count) ^ col_index]
    else:
        corner = lax.all_gather(corner, "cols")

    solved, solved_high, solved_low = solve_rows(
        jnp.stack([core]), own_head, other_head, first_inverse, corner
    )
    is_top = (row_index * BLOCK < depth).astype(jnp.int32)
    own_block = jnp.minimum(row_index, depth // BLOCK - 1)

    slab = window_slab.reshape(col_count, piece, breadth)
    updated, done, results, ready = [], [], [], []

    def update(j):
        number = next(g for g, group in enumerate(groups) if j in group)
        after = [done[j - 1 if j == 4 else j - AHEAD]] if j >= AHEAD else ready
        after = after + (updated[2][1][1:2] if j == 3 else [])
        out = update_rows(
            jnp.stack([col_index, own_block, is_top]),
            slab,
            factors[number],
            solved_high,
            solved_low,
            solved,
            begins[j],
            sizes[j],
            begins[j] - begins[groups[number][0]],
            after,
        )
        pieces = [out[0]]
        for slot in range(1, col_count):
            pieces.append(lax.ppermute(out[slot], "cols", over_cols[slot]))
        updated.append((out, pieces))

    update(0)

    own_second = gate(own_second, [updated[0][0][0]])
    other_second = from_sibling(own_second)
    place_cores = jnp.stack([col_index, core])
    ready = [own_second]
    if chunks > 1:
        update(1)
    factors += [gather_factor(group, ready) for group in groups[1:]]

    for j in range(chunks):
        pieces = updated[j][1]
        after = [updated[j + 1][0][0]] if j + 1 < len(updated) else []
        after += [results[j - 2]] if j >= 2 else []
        after += factors[2:] if j == 3 else []
        done.append(
            reduce_columns(
                place_cores, pieces, second_inverse, own_second, other_second, row_count, after
            )
        )
        results.append(lax.all_to_all(done[j], "rows", split_axis=0, concat_axis=0, tiled=True))
        stop = j + AHEAD + (1 if j != 2 else 0)
        for later in range(len(updated), min(stop if j else AHEAD + 1, chunks)):
            update(later)
            if later == 2:
                factors[2] = gather_factor(groups[2], updated[2][1][1:2])
    turned = jnp.concatenate(results, 1)
    return turned.reshape(row_count * piece, narrow)


def solution(mesh):
    return jax.shard_map(
        on_device,
        mesh=mesh,
        in_specs=(P("rows", "cols"), P(), P(None, "cols", "rows"), P(), P(None, "cols", "rows")),
        out_specs=P("cols", "rows"),
        check_vma=False,
    )
```
